32 devices in a mesh: expert: 8 (over z, x), mp: 4 (over y, core).
Axes of the slice: x: 2, y: 2, z: 4, core: 2. Of those that a mesh axis runs over, the one named last changes fastest.
Arguments:
- stream: bfloat16 [4096, 2048], P(('expert', 'mp')), may hold values from -60 to 60
- attn_gain: float32 [2048], replicated, may hold values from 0.5 to 1.5
- routes: int32 [4096, 6], P(('expert', 'mp')), may hold values from 0 to 15, as said below
- route_weights: float32 [4096, 6], P(('expert', 'mp')), may hold values from 0.05 to 0.4
- segment_ids: int32 [4096], P(('expert', 'mp')), may hold values from 0 to 3, never falling along the last dimension, each value on 1 to 2048 neighbouring positions
- gate_weight: bfloat16 [32, 2048, 704], P(('expert', 'mp')), may hold values from -0.125 to 0.125
- up_weight: bfloat16 [32, 2048, 704], P(('expert', 'mp')), may hold values from -1 to 1
- down_weight: bfloat16 [32, 1408, 1024], P(('expert', 'mp')), may hold values from -0.15625 to 0.15625
- keep_channels: int32 [16, 1024], replicated, may hold values from 0 to 1407, as said below
- next_gain: float32 [2048], replicated, may hold values from 0.5 to 1.5
- kv_down: bfloat16 [2048, 512], replicated, may hold values from -0.125 to 0.125
- rope_down: bfloat16 [2048, 64], replicated, may hold values from -0.125 to 0.125
- kv_gain: float32 [512], replicated, may hold values from 0.5 to 1.5
Outputs:
- moe_out: bfloat16 [4096, 2048], P(('expert', 'mp'))
- latent: bfloat16 [4096, 512], P(('expert', 'mp'))
- rope_key: bfloat16 [4096, 64], P(('expert', 'mp'))
The draws below stay inside these ranges and needn't reach their ends.
Inputs may be any that keep to these rules, and one draw needn't show every extreme that they name: `routes`: in the 128 rows of each device (aligned blocks of the token order) each row names 6 different experts, no expert is named by more than 72 rows, every expert is named at least once, and one expert, the same on every device, is named by exactly 72 rows. `keep_channels`: each row holds 1024 different hidden units. `segment_ids`: segment ids never fall along the tokens.
All inputs are finite; a program needn't handle non-finite values.
Results may differ from the reference program's by a relative error of at most 0.012.
Values may be sent and summed in bfloat16 or wider, within the bound.
A program may use at most 128 MiB of HBM per device.

```python
import math
import jax
import jax.numpy as jnp
import numpy as np
from jax import lax

D = 2048
FF = 1408
TOP = 6
LATENT = 512
ROPE = 64
KEEP = 1024
TOK_DEV = 128
EXPERTS = 16
CAP = 72
TOKENS = 4096
SEQ = 2048
NSEQ = 4
N_EXPERT = 8
N_MP = 4


def draw_stream(key, part):
    base_key, row_key, column_key = jax.random.split(jax.random.fold_in(key, 31), 3)
    base = jnp.clip(jax.random.normal(base_key, (TOKENS, D)), -6.0, 6.0)
    row_scale = jnp.exp(jax.random.uniform(row_key, (TOKENS, 1), minval=-1.15, maxval=1.15))
    column_scale = jnp.exp(jax.random.uniform(column_key, (1, D), minval=-1.15, maxval=1.15))
    values = base * row_scale * column_scale
    return jnp.clip(values, -60.0, 60.0).astype(jnp.bfloat16)


def draw_up_weight(key, part):
    base_key, column_key = jax.random.split(jax.random.fold_in(key, 41))
    shape = (2 * EXPERTS, D, FF // 2)
    base = jnp.clip(jax.random.normal(base_key, shape), -6.0, 6.0)
    column_scale = jnp.exp(jax.random.uniform(column_key, (2 * EXPERTS, 1, FF // 2), minval=-1.15, maxval=1.15))
    values = base * column_scale / jnp.sqrt(jnp.float32(D))
    return jnp.clip(values, -1.0, 1.0).astype(jnp.bfloat16)


def draw_keep_channels(key, part):
    expert_keys = jax.random.split(jax.random.fold_in(key, 21), EXPERTS)

    def one_expert(expert_key):
        return jax.random.permutation(expert_key, FF)[:KEEP]
    return jax.vmap(one_expert)(expert_keys).astype(jnp.int32)


def draw_routes(key, part):
    blocks = TOKENS // TOK_DEV
    spare = EXPERTS - 1
    slots = spare * (CAP - 1)
    extra_total = TOP * TOK_DEV - CAP - spare
    hot_expert = jax.random.randint(jax.random.fold_in(key, 11), (), 0, EXPERTS)
    block_keys = jax.random.split(jax.random.fold_in(key, 12), blocks)
    spare_index = jnp.arange(spare, dtype=jnp.int32)
    others = spare_index + (spare_index >= hot_expert).astype(jnp.int32)

    def one_block(block_key):
        bias_key, noise_key, order_key, token_key = jax.random.split(block_key, 4)
        bias = jax.random.randint(bias_key, (spare, 1), 0, 1024)
        noise = jax.random.randint(noise_key, (spare, CAP - 1), 0, 1024)
        score = ((bias + noise).reshape(-1) * slots + jnp.arange(slots, dtype=jnp.int32)).astype(jnp.int32)
        picked = lax.top_k(score, extra_total)[1]
        extra = jnp.zeros((spare,), jnp.int32).at[picked // (CAP - 1)].add(1)
        counts = jnp.zeros((EXPERTS,), jnp.int32).at[others].set(1 + extra).at[hot_expert].set(CAP)
        order = jax.random.permutation(order_key, EXPERTS).astype(jnp.int32)
        labels = jnp.repeat(order, jnp.take(counts, order), total_repeat_length=TOP * TOK_DEV)
        table = labels.reshape(TOP, TOK_DEV).T
        shuffle = jax.random.permutation(token_key, TOK_DEV)
        return jnp.take(table, shuffle, axis=0)
    return jax.vmap(one_block)(block_keys).reshape(TOKENS, TOP).astype(jnp.int32)


def block_levels(key, extent, cuts, low, high):
    gain, own = 1.0, jax.random.fold_in(key, 6)
    for axis_at, shards_of in cuts:
        steps = jnp.exp(jax.random.uniform(jax.random.fold_in(own, axis_at), (shards_of,), jnp.float32, low / len(cuts), high / len(cuts)))
        gain = gain * jnp.repeat(steps, extent[axis_at] // shards_of).reshape([-1 if axis == axis_at else 1 for axis in range(len(extent))])
    return gain


def split_up(number_of, total, limit, slope):
    portions = [(1 << 20) // math.isqrt(standing ** slope) + 1 for standing in range(2, number_of + 1)]
    rest, holding = total - limit - (number_of - 1), [1] * (number_of - 1)
    while rest > 0:
        free = [i for i in range(number_of - 1) if holding[i] < limit]
        whole, left = sum([portions[i] for i in free]), rest
        for i in free:
            more = min(limit - holding[i], max(1, left * portions[i] // whole), rest)
            holding[i] = holding[i] + more
            rest = rest - more
    return np.array([limit] + holding)


def uneven(key, amount, total, limit, skew):
    if amount == 2:
        one = jax.random.randint(key, (), max(1, total - limit), min(limit, total - 1) + 1)
        return jnp.stack([one, total - one])
    lengths = jnp.asarray(split_up(amount, total, limit, skew), jnp.int32)
    pairs = (amount - 1) // 2
    donor, receiver = lengths[1:1 + 2 * pairs:2], lengths[2:2 + 2 * pairs:2]
    margin = jnp.minimum(donor - 1, limit - receiver)
    shifted = jax.random.randint(jax.random.fold_in(key, 1), (pairs,), 0, 1 << 20) % (margin + 1)
    lengths = lengths.at[1:1 + 2 * pairs:2].set(donor - shifted).at[2:2 + 2 * pairs:2].set(receiver + shifted)
    return lengths[jax.random.permutation(jax.random.fold_in(key, 2), amount)]


def centred(key, dims, deviation, limit, pieces=(), kind=jnp.bfloat16):
    factor_of = block_levels(key, dims, pieces, -0.22, 0.18) if pieces else 1.0
    drawn = jax.random.normal(key, dims, jnp.float32) * deviation * factor_of
    return jnp.minimum(jnp.maximum(drawn, -limit), limit).astype(kind)


def setup_inputs(seed: int = 0) -> dict:
    keys = jax.random.split(jax.random.key(seed), 14)
    return {
        "stream": draw_stream(jax.random.fold_in(keys[13], 71), 0),
        "attn_gain": jnp.clip(1.0 + 0.1 * jax.random.normal(keys[1], (D,), jnp.float32), 0.5, 1.5),
        "routes": draw_routes(jax.random.fold_in(keys[13], 71), 0),
        "route_weights": jnp.clip(0.05 + 0.35 * jax.random.uniform(keys[3], (TOKENS, TOP), jnp.float32) ** block_levels(keys[3], (TOKENS, TOP), ((0, 32),), -0.2, 0.2), 0.05, 0.4),
        "segment_ids": jnp.searchsorted(jnp.cumsum(uneven(keys[4], NSEQ, TOKENS, SEQ, 1)), jnp.arange(TOKENS), side="right").astype(jnp.int32),
        "gate_weight": centred(keys[5], (2 * EXPERTS, D, FF // 2), D ** -0.5, 0.125, ((0, 32),)),
        "up_weight": draw_up_weight(jax.random.fold_in(keys[13], 71), 0),
        "down_weight": centred(keys[7], (2 * EXPERTS, FF, D // 2), FF ** -0.5, 0.15625, ((0, 32),)),
        "keep_channels": draw_keep_channels(jax.random.fold_in(keys[13], 71), 0),
        "next_gain": jnp.clip(1.0 + 0.1 * jax.random.normal(keys[9], (D,), jnp.float32), 0.5, 1.5),
        "kv_down": centred(keys[10], (D, LATENT), D ** -0.5, 0.125),
        "rope_down": centred(keys[11], (D, ROPE), D ** -0.5, 0.125),
        "kv_gain": jnp.clip(1.0 + 0.1 * jax.random.normal(keys[12], (LATENT,), jnp.float32), 0.5, 1.5),
    }


EPSILON = 1e-06
DAMPING = 0.05
ROPE_BASE = 10000.0

def rms_rows(values, scale_gain):
    mean_square = lax.optimization_barrier(jnp.mean(values * values, axis=-1, keepdims=True))
    return values * lax.rsqrt(mean_square + EPSILON) * scale_gain

def rotate(rope_in, position):
    half_width = rope_in.shape[1] // 2
    frequency = jnp.exp(jnp.arange(half_width, dtype=jnp.float32) * (-2.0 * math.log(ROPE_BASE) / rope_in.shape[1]))
    angles = position[:, None] * frequency[None, :]
    first_half = rope_in[:, :half_width]
    second_half = rope_in[:, half_width:]
    cosine = jnp.cos(angles)
    sine = jnp.sin(angles)
    return jnp.concatenate([first_half * cosine - second_half * sine, second_half * cosine + first_half * sine], axis=1)

def split_target(cross_gram, down_full):
    cross_high = lax.optimization_barrier(cross_gram.astype(jnp.bfloat16))
    cross_low = (cross_gram - cross_high.astype(jnp.float32)).astype(jnp.bfloat16)
    high_part = jnp.dot(cross_high.astype(jnp.float32), down_full.astype(jnp.float32), preferred_element_type=jnp.float32)
    low_part = jnp.dot(cross_low.astype(jnp.float32), down_full.astype(jnp.float32), preferred_element_type=jnp.float32)
    return high_part + low_part

def reference(stream, attn_gain, routes, route_weights, segment_ids, gate_weight, up_weight, down_weight, keep_channels, next_gain, kv_down, rope_down, kv_gain):
    stream_f = stream.astype(jnp.float32)
    moe_input = rms_rows(stream_f, attn_gain).astype(jnp.bfloat16)
    max_rows = N_EXPERT * N_MP * CAP
    contract_dims = (((0,), (0,)), ((), ()))

    def expert_step(moe_total, expert):
        chosen = routes == expert
        routed = jnp.any(chosen, axis=1)
        row_index = jnp.nonzero(routed, size=max_rows, fill_value=0)[0].astype(jnp.int32)
        live_count = jnp.sum(routed.astype(jnp.int32))
        live_rows = jnp.arange(max_rows, dtype=jnp.int32) < live_count
        picked = jnp.take(moe_input, row_index, axis=0) * live_rows.astype(jnp.bfloat16)[:, None]
        pair_index = 2 * expert
        gate_full = jnp.concatenate([gate_weight[pair_index], gate_weight[pair_index + 1]], axis=1)
        up_full = jnp.concatenate([up_weight[pair_index], up_weight[pair_index + 1]], axis=1)
        gate_proj = jnp.dot(picked.astype(jnp.float32), gate_full.astype(jnp.float32), preferred_element_type=jnp.float32)
        up_proj = jnp.dot(picked.astype(jnp.float32), up_full.astype(jnp.float32), preferred_element_type=jnp.float32)
        hidden = (jax.nn.silu(gate_proj) * up_proj).astype(jnp.bfloat16)
        kept_index = keep_channels[expert].astype(jnp.int32)
        kept = jnp.take(hidden, kept_index, axis=1)
        cross_gram = lax.dot_general(kept.astype(jnp.float32), hidden.astype(jnp.float32), contract_dims, preferred_element_type=jnp.float32)
        inner_gram = jnp.take(cross_gram, kept_index, axis=1)
        damping_term = DAMPING * jnp.mean(jnp.diagonal(inner_gram))
        system = inner_gram + damping_term * jnp.eye(inner_gram.shape[0], dtype=jnp.float32)
        factor = jnp.linalg.cholesky(system)
        down_full = jnp.concatenate([down_weight[pair_index], down_weight[pair_index + 1]], axis=1)
        target_cols = split_target(cross_gram, down_full)
        pruned = jax.scipy.linalg.cho_solve((factor, True), target_cols).astype(jnp.bfloat16)
        refit = jnp.dot(kept.astype(jnp.float32), pruned.astype(jnp.float32), preferred_element_type=jnp.float32).astype(jnp.bfloat16)
        row_weight = lax.optimization_barrier(jnp.sum(jnp.where(chosen, route_weights, jnp.zeros_like(route_weights)), axis=1))
        weight_rows = jnp.take(row_weight, row_index) * live_rows.astype(route_weights.dtype)
        moe_total = moe_total.at[row_index].add(weight_rows[:, None] * refit.astype(jnp.float32))
        return (moe_total, None)
    moe_total, unused = lax.scan(expert_step, jnp.zeros((TOKENS, D), jnp.float32), jnp.arange(EXPERTS, dtype=jnp.int32))
    moe_out = moe_total.astype(jnp.bfloat16)
    next_stream = (stream_f + moe_out.astype(jnp.float32)).astype(jnp.bfloat16)
    normed = rms_rows(next_stream.astype(jnp.float32), next_gain).astype(jnp.bfloat16)
    compressed = jnp.dot(normed.astype(jnp.float32), kv_down.astype(jnp.float32), preferred_element_type=jnp.float32)
    latent = rms_rows(compressed, kv_gain).astype(jnp.bfloat16)
    rope_in = jnp.dot(normed.astype(jnp.float32), rope_down.astype(jnp.float32), preferred_element_type=jnp.float32)
    seq_hits = (segment_ids[:, None] == jnp.arange(NSEQ, dtype=jnp.int32)[None, :]).astype(jnp.int32)
    counts = lax.optimization_barrier(jnp.sum(seq_hits, axis=0))
    starts = jnp.cumsum(counts) - counts
    position = jnp.arange(TOKENS, dtype=jnp.int32) - jnp.take(starts, segment_ids.astype(jnp.int32))
    rope_key = rotate(rope_in, position.astype(jnp.float32)).astype(jnp.bfloat16)
    return (moe_out, latent, rope_key)
```

```python
import functools
import math

import jax
import jax.numpy as jnp
from jax import lax
from jax.experimental import pallas as pl
from jax.experimental.pallas import tpu as pltpu
from jax.sharding import Mesh
from jax.sharding import PartitionSpec as P

TOP = 6
EPSILON = 1e-06
DAMPING = 0.05
ROPE_BASE = 10000.0
BLOCK = 128
SUB = 8
CHIPS = ("expert", "y")
DEVICES = ("expert", "y", "core")


def rms_rows(values, scale_gain):
    mean_square = jnp.mean(values * values, axis=-1, keepdims=True)
    return values * lax.rsqrt(mean_square + EPSILON) * scale_gain


def rotate(rope_in, position):
    half_width = rope_in.shape[1] // 2
    frequency = jnp.exp(
        jnp.arange(half_width, dtype=jnp.float32) * (-2.0 * math.log(ROPE_BASE) / rope_in.shape[1])
    )
    angles = position[:, None] * frequency[None, :]
    first_half = rope_in[:, :half_width]
    second_half = rope_in[:, half_width:]
    cosine = jnp.cos(angles)
    sine = jnp.sin(angles)
    return jnp.concatenate(
        [first_half * cosine - second_half * sine, second_half * cosine + first_half * sine], axis=1
    )


def precise_dot(a, b):
    return jnp.dot(a, b, precision=lax.Precision.HIGHEST, preferred_element_type=jnp.float32)


def sweep_panel(panel, row_id, lane_id):
    for q in range(0, SUB, 2):
        c0 = jnp.broadcast_to(panel[:, q : q + 1], panel.shape)
        c1 = jnp.broadcast_to(panel[:, q + 1 : q + 2], panel.shape)
        r0 = jnp.broadcast_to(panel[q : q + 1, :], panel.shape)
        r1 = jnp.broadcast_to(panel[q + 1 : q + 2, :], panel.shape)
        a = jnp.broadcast_to(c0[q : q + 1, :], panel.shape)
        b = jnp.broadcast_to(c1[q : q + 1, :], panel.shape)
        d = jnp.broadcast_to(c1[q + 1 : q + 2, :], panel.shape)
        inverse = 1.0 / (a * d - b * b)
        i00, i01, i11 = d * inverse, -b * inverse, a * inverse
        at0, at1 = lane_id == q, lane_id == q + 1
        r0 = jnp.where(at0, 1.0, jnp.where(at1, 0.0, r0))
        r1 = jnp.where(at1, 1.0, jnp.where(at0, 0.0, r1))
        s0 = i00 * r0 + i01 * r1
        s1 = i01 * r0 + i11 * r1
        swept = jnp.where(at0 | at1, 0.0, panel) - c0 * s0 - c1 * s1
        panel = jnp.where(row_id == q, s0, jnp.where(row_id == q + 1, s1, swept))
    return panel


def sweep_step(rows):
    row_id = lax.broadcasted_iota(jnp.int32, (SUB, BLOCK), 0)
    lane_id = lax.broadcasted_iota(jnp.int32, (SUB, BLOCK), 1)
    done = sweep_panel(rows[0], row_id, lane_id)
    spread = [jnp.broadcast_to(done[q : q + 1, :], done.shape) for q in range(SUB)]
    out = []
    for row in rows[1:]:
        left = jnp.where(lane_id < SUB, 0.0, row)
        terms = [jnp.broadcast_to(row[:, q : q + 1], row.shape) * spread[q] for q in range(SUB)]
        while len(terms) > 1:
            terms = [terms[i] + terms[i + 1] for i in range(0, len(terms), 2)]
        out.append(left - terms[0])
    out.append(done)
    return tuple(pltpu.roll(row, BLOCK - SUB, 1) for row in out)


def solve_kernel(inner_ref, target_ref, out_ref, work, gain):
    size = inner_ref.shape[0]
    width = target_ref.shape[1]
    blocks = size // BLOCK
    eye = lax.broadcasted_iota(jnp.int32, (BLOCK, BLOCK), 0) == lax.broadcasted_iota(
        jnp.int32, (BLOCK, BLOCK), 1
    )
    trace = jnp.zeros((BLOCK, BLOCK), jnp.float32)
    for k in range(blocks):
        at = pl.ds(k * BLOCK, BLOCK)
        trace = trace + jnp.where(eye, inner_ref[at, at], 0.0)
    total = jnp.sum(jnp.sum(trace, axis=1, keepdims=True), axis=0, keepdims=True)
    scale = size / total

    @pl.loop(0, size // 32)
    def _(i):
        at = pl.ds(pl.multiple_of(i * 32, 32), 32)
        work[at, :size] = inner_ref[at, :] * scale
        work[at, size:] = target_ref[at, :] * scale

    for k in range(blocks):
        at = pl.ds(k * BLOCK, BLOCK)
        low = (k + 1) * BLOCK
        square = work[at, at] + jnp.where(eye, DAMPING, 0.0)
        rows = tuple(square[SUB * i : SUB * (i + 1), :] for i in range(BLOCK // SUB))
        rows = lax.fori_loop(0, BLOCK // SUB, lambda _, rows: sweep_step(rows), rows)
        inverse = jnp.concatenate(rows, axis=0)
        tile = 512 if low % 512 == 0 else (256 if low % 256 == 0 else BLOCK)

        def column(start, tile, low=low, at=at, inverse=inverse):
            cols = pl.ds(start, tile)
            solved = precise_dot(inverse, work[at, cols])
            gain[at, cols] = solved
            if low < size:
                work[low:, cols] -= precise_dot(work[low:, at], solved)

        start = low
        while start % 512:
            column(start, BLOCK)
            start += BLOCK

        @pl.loop(0, (size + width - start) // 512)
        def _(i, start=start, column=column):
            column(pl.multiple_of(start + i * 512, 512), 512)

    @pl.loop(0, width // 256)
    def _(i):
        start = pl.multiple_of(i * 256, 256)
        cols = pl.ds(pl.multiple_of(size + start, 256), 256)
        for k in reversed(range(blocks)):
            at = pl.ds(k * BLOCK, BLOCK)
            low = (k + 1) * BLOCK
            value = gain[at, cols]
            if low < size:
                value = value - precise_dot(gain[at, low:size], work[low:, cols])
            work[at, cols] = value
        out_ref[:, pl.ds(start, 256)] = work[:, cols].astype(out_ref.dtype)


def damped_solve(inner, target):
    size, width = inner.shape[0], target.shape[1]
    return pl.pallas_call(
        solve_kernel,
        out_shape=jax.ShapeDtypeStruct((size, width), jnp.bfloat16),
        in_specs=[pl.BlockSpec(memory_space=pltpu.VMEM)] * 2,
        out_specs=pl.BlockSpec(memory_space=pltpu.VMEM),
        scratch_shapes=[
            pltpu.VMEM((size, size + width), jnp.float32),
            pltpu.VMEM((size, size + width), jnp.float32),
        ],
        compiler_params=pltpu.CompilerParams(vmem_limit_bytes=48 * 2**20),
        cost_estimate=pl.CostEstimate(
            flops=6 * size * size * width, bytes_accessed=10 * size * width, transcendentals=0
        ),
    )(inner, target)


def split_target(cross_gram, down_part):
    cross_high = lax.optimization_barrier(cross_gram.astype(jnp.bfloat16))
    cross_low = (cross_gram - cross_high.astype(jnp.float32)).astype(jnp.bfloat16)
    high_part = jnp.dot(cross_high, down_part, preferred_element_type=jnp.float32)
    low_part = jnp.dot(cross_low, down_part, preferred_element_type=jnp.float32)
    return high_part + low_part


def both_halves(value, core):
    other = lax.ppermute(value, "core", [(0, 1), (1, 0)])
    return jnp.where(
        core == 0,
        jnp.concatenate([value, other], axis=1),
        jnp.concatenate([other, value], axis=1),
    )


def local(
    stream,
    attn_gain,
    routes,
    route_weights,
    segment_ids,
    gate_weight,
    up_weight,
    down_weight,
    keep_channels,
    next_gain,
    kv_down,
    rope_down,
    kv_gain,
):
    f32, bf16 = jnp.float32, jnp.bfloat16
    tok_rows = stream.shape[0]
    chips = lax.axis_size(CHIPS)
    devices = 2 * chips
    experts = chips
    capacity = max(2, 3 * tok_rows * TOP // (2 * experts))
    core = lax.axis_index("core")
    expert_id = lax.axis_index(CHIPS)
    stream_f = stream.astype(f32)
    moe_input = rms_rows(stream_f, attn_gain).astype(bf16)
    half_width = down_weight.shape[2]
    model_width = stream.shape[1]

    gathered = lax.all_gather(moe_input, CHIPS, tiled=True).reshape(chips, tok_rows, model_width)
    gate_full = both_halves(gate_weight[0], core)
    up_full = both_halves(up_weight[0], core)

    token_total = tok_rows * devices
    seq_length = min(2048, token_total // 2)
    sequences = 2 * token_total // seq_length
    seq_hits = segment_ids[:, None] == jnp.arange(sequences, dtype=jnp.int32)[None, :]
    local_counts = jnp.sum(seq_hits.astype(f32), axis=0)
    count_row = jnp.pad(local_counts, (0, tok_rows - sequences))[None, :]
    packed_routes = jnp.concatenate([routes.T.astype(f32), route_weights.T, count_row], axis=0)
    all_routes = lax.all_gather(packed_routes, DEVICES)
    chosen = all_routes[:, :TOP] == expert_id.astype(f32)
    weight_rows = jnp.sum(jnp.where(chosen, all_routes[:, TOP : 2 * TOP], 0.0), axis=1)
    hits = jnp.any(chosen, axis=1)
    token_order = jnp.arange(tok_rows, dtype=jnp.int32)
    earlier = (token_order[:, None] < token_order[None, :]).astype(bf16)
    slots = jnp.dot(hits.astype(bf16), earlier, preferred_element_type=f32)
    slots = jnp.where(hits, slots, -1.0)
    slot_ids = jnp.arange(capacity, dtype=jnp.int32).astype(f32)
    by_core = slots.reshape(chips, 2, tok_rows)
    slots_mine = lax.dynamic_index_in_dim(by_core, core, 1, keepdims=False)
    slots_other = lax.dynamic_index_in_dim(by_core, 1 - core, 1, keepdims=False)
    weights_by_core = weight_rows.reshape(chips, 2, tok_rows)

    pick = (slots_mine[:, None, :] == slot_ids[None, :, None]).astype(bf16)
    picked = jnp.einsum("bct,btd->bcd", pick, gathered, preferred_element_type=f32).astype(bf16)
    picked = picked.reshape(chips * capacity, model_width)
    gate_proj = jnp.dot(picked, gate_full, preferred_element_type=f32)
    up_proj = jnp.dot(picked, up_full, preferred_element_type=f32)
    hidden_mine = (jax.nn.silu(gate_proj) * up_proj).astype(bf16)
    hidden_other = lax.ppermute(hidden_mine, "core", [(0, 1), (1, 0)])

    kept_index = lax.dynamic_slice_in_dim(keep_channels, expert_id, 1, 0)[0]
    unit_ids = jnp.arange(hidden_mine.shape[1], dtype=jnp.int32)
    select = (unit_ids[:, None] == kept_index[None, :]).astype(bf16)
    kept_mine = jnp.dot(hidden_mine, select, preferred_element_type=f32).astype(bf16)
    kept_other = jnp.dot(hidden_other, select, preferred_element_type=f32).astype(bf16)
    contract = (((0,), (0,)), ((), ()))
    gram = functools.partial(
        lax.dot_general, dimension_numbers=contract, preferred_element_type=f32
    )
    cross_gram = gram(kept_mine, hidden_mine) + gram(kept_other, hidden_other)
    inner_gram = gram(kept_mine, kept_mine) + gram(kept_other, kept_other)
    target_cols = split_target(cross_gram, down_weight[0])
    pruned = damped_solve(inner_gram, target_cols)

    def weighted(kept, slot_rows, weights):
        refit = jnp.dot(kept, pruned, preferred_element_type=f32).astype(bf16)
        place = slot_rows[:, None, :] == slot_ids[None, :, None]
        slot_weights = jnp.sum(jnp.where(place, weights[:, None, :], 0.0), axis=2)
        rows = refit.astype(f32) * slot_weights.reshape(-1)[:, None]
        return rows.astype(bf16).reshape(chips, capacity, half_width)

    weights_mine = lax.dynamic_index_in_dim(weights_by_core, core, 1, keepdims=False)
    weights_other = lax.dynamic_index_in_dim(weights_by_core, 1 - core, 1, keepdims=False)
    rows_mine = weighted(kept_mine, slots_mine, weights_mine)
    rows_other = weighted(kept_other, slots_other, weights_other)
    outgoing = jnp.stack(
        [jnp.where(core == 0, rows_mine, rows_other), jnp.where(core == 0, rows_other, rows_mine)],
        axis=1,
    ).reshape(devices, capacity, half_width)
    returned = lax.all_to_all(outgoing, DEVICES, split_axis=0, concat_axis=0, tiled=True)
    returned = returned.reshape(experts, 2, capacity, half_width)
    expert_range = jnp.arange(experts, dtype=jnp.int32)
    local_hits = jnp.any(routes[:, :, None] == expert_range[None, None, :], axis=1)
    local_slots = jnp.dot(earlier.T, local_hits.astype(bf16), preferred_element_type=f32)
    local_slots = jnp.where(local_hits, local_slots, -1.0)
    combine = (local_slots[:, :, None] == slot_ids[None, None, :]).astype(bf16)
    moe_sum = jnp.einsum("tec,ehcd->thd", combine, returned, preferred_element_type=f32)
    moe_out = moe_sum.reshape(tok_rows, model_width).astype(bf16)

    counts = jnp.sum(all_routes[:, 2 * TOP, :sequences], axis=0)
    sequence_range = jnp.arange(sequences, dtype=jnp.int32)
    before = sequence_range[None, :] < sequence_range[:, None]
    starts = jnp.sum(jnp.where(before, counts[None, :], 0.0), axis=1)
    token_start = jnp.sum(jnp.where(seq_hits, starts[None, :], 0.0), axis=1)
    global_index = (
        lax.axis_index(DEVICES) * tok_rows + jnp.arange(tok_rows, dtype=jnp.int32)
    ).astype(f32)
    position = global_index - token_start

    next_stream = (stream_f + moe_out.astype(f32)).astype(bf16)
    normed = rms_rows(next_stream.astype(f32), next_gain).astype(bf16)
    compressed = jnp.dot(normed, kv_down, preferred_element_type=f32)
    latent = rms_rows(compressed, kv_gain).astype(bf16)
    rope_in = jnp.dot(normed, rope_down, preferred_element_type=f32)
    rope_key = rotate(rope_in, position).astype(bf16)
    return (moe_out, latent, rope_key)


def solution(mesh):
    chips_mesh = Mesh(
        mesh.devices.reshape(mesh.shape["expert"], mesh.shape["mp"] // 2, 2), DEVICES
    )
    split = P(DEVICES)
    in_specs = (split, P(), split, split, split, split, split, split, P(), P(), P(), P(), P())
    return jax.shard_map(
        local, mesh=chips_mesh, in_specs=in_specs, out_specs=(split,) * 3, check_vma=False
    )
```

```python
import functools
import math

import jax
import jax.numpy as jnp
from jax import lax
from jax.experimental import pallas as pl
from jax.experimental.pallas import tpu as pltpu
from jax.sharding import Mesh
from jax.sharding import PartitionSpec as P

TOP = 6
EPSILON = 1e-06
DAMPING = 0.05
ROPE_BASE = 10000.0
BLOCK = 128
SUB = 8
CHIPS = ("expert", "y")
DEVICES = ("expert", "y", "core")


def rms_rows(values, scale_gain):
    mean_square = jnp.mean(values * values, axis=-1, keepdims=True)
    return values * lax.rsqrt(mean_square + EPSILON) * scale_gain


def rotate(rope_in, position):
    half_width = rope_in.shape[1] // 2
    frequency = jnp.exp(
        jnp.arange(half_width, dtype=jnp.float32) * (-2.0 * math.log(ROPE_BASE) / rope_in.shape[1])
    )
    angles = position[:, None] * frequency[None, :]
    first_half = rope_in[:, :half_width]
    second_half = rope_in[:, half_width:]
    cosine = jnp.cos(angles)
    sine = jnp.sin(angles)
    return jnp.concatenate(
        [first_half * cosine - second_half * sine, second_half * cosine + first_half * sine], axis=1
    )


def precise_dot(a, b):
    return jnp.dot(a, b, precision=lax.Precision.HIGHEST, preferred_element_type=jnp.float32)


def sweep_panel(panel, row_id, lane_id):
    for q in range(0, SUB, 2):
        c0 = jnp.broadcast_to(panel[:, q : q + 1], panel.shape)
        c1 = jnp.broadcast_to(panel[:, q + 1 : q + 2], panel.shape)
        r0 = jnp.broadcast_to(panel[q : q + 1, :], panel.shape)
        r1 = jnp.broadcast_to(panel[q + 1 : q + 2, :], panel.shape)
        a = jnp.broadcast_to(c0[q : q + 1, :], panel.shape)
        b = jnp.broadcast_to(c1[q : q + 1, :], panel.shape)
        d = jnp.broadcast_to(c1[q + 1 : q + 2, :], panel.shape)
        inverse = 1.0 / (a * d - b * b)
        i00, i01, i11 = d * inverse, -b * inverse, a * inverse
        at0, at1 = lane_id == q, lane_id == q + 1
        r0 = jnp.where(at0, 1.0, jnp.where(at1, 0.0, r0))
        r1 = jnp.where(at1, 1.0, jnp.where(at0, 0.0, r1))
        s0 = i00 * r0 + i01 * r1
        s1 = i01 * r0 + i11 * r1
        swept = jnp.where(at0 | at1, 0.0, panel) - c0 * s0 - c1 * s1
        panel = jnp.where(row_id == q, s0, jnp.where(row_id == q + 1, s1, swept))
    return panel


def sweep_step(rows):
    row_id = lax.broadcasted_iota(jnp.int32, (SUB, BLOCK), 0)
    lane_id = lax.broadcasted_iota(jnp.int32, (SUB, BLOCK), 1)
    done = sweep_panel(rows[0], row_id, lane_id)
    spread = [jnp.broadcast_to(done[q : q + 1, :], done.shape) for q in range(SUB)]
    out = []
    for row in rows[1:]:
        left = jnp.where(lane_id < SUB, 0.0, row)
        terms = [jnp.broadcast_to(row[:, q : q + 1], row.shape) * spread[q] for q in range(SUB)]
        while len(terms) > 1:
            terms = [terms[i] + terms[i + 1] for i in range(0, len(terms), 2)]
        out.append(left - terms[0])
    out.append(done)
    return tuple(pltpu.roll(row, BLOCK - SUB, 1) for row in out)


def in_three(value):
    high = value.astype(jnp.bfloat16)
    rest = value - high.astype(jnp.float32)
    middle = rest.astype(jnp.bfloat16)
    return high, middle, (rest - middle.astype(jnp.float32)).astype(jnp.bfloat16)


def solve_kernel(inner_ref, target_ref, out_ref, work, near, far):
    size = inner_ref.shape[0]
    width = target_ref.shape[1]
    blocks = size // BLOCK
    eye = lax.broadcasted_iota(jnp.int32, (BLOCK, BLOCK), 0) == lax.broadcasted_iota(
        jnp.int32, (BLOCK, BLOCK), 1
    )
    trace = jnp.zeros((BLOCK, BLOCK), jnp.float32)
    for k in range(blocks):
        at = pl.ds(k * BLOCK, BLOCK)
        trace = trace + jnp.where(eye, inner_ref[at, at], 0.0)
    total = jnp.sum(jnp.sum(trace, axis=1, keepdims=True), axis=0, keepdims=True)
    scale = size / total

    @pl.loop(0, size // 32)
    def _(i):
        at = pl.ds(pl.multiple_of(i * 32, 32), 32)
        work[at, :size] = inner_ref[at, :] * scale
        work[at, size:] = target_ref[at, :] * scale

    def diagonal_rows(k):
        at = pl.ds(k * BLOCK, BLOCK)
        square = work[at, at] + jnp.where(eye, DAMPING, 0.0)
        return tuple(square[SUB * i : SUB * (i + 1), :] for i in range(BLOCK // SUB))

    def two_steps(rows):
        return sweep_step(sweep_step(rows))

    pairs = BLOCK // SUB // 2
    rows = lax.fori_loop(0, pairs, lambda _, rows: two_steps(rows), diagonal_rows(0))
    for k in range(blocks):
        at = pl.ds(k * BLOCK, BLOCK)
        low = (k + 1) * BLOCK
        inverse = jnp.concatenate(rows, axis=0)
        high, middle, small = in_three(work[:, at])
        near[:, :BLOCK] = high
        near[:, BLOCK:] = middle
        far[:, :BLOCK] = high
        far[:, BLOCK:] = small
        ranges = [r for r in ((0, k * BLOCK), (low, size)) if r[0] < r[1]]

        def column(start, tile, at=at, inverse=inverse, ranges=ranges):
            cols = pl.ds(start, tile)
            solved = precise_dot(inverse, work[at, cols])
            b0, b1, b2 = in_three(solved)
            b00 = jnp.concatenate([b0, b0], axis=0)
            b11 = jnp.concatenate([b1, b1], axis=0)
            b20 = jnp.concatenate([b2, b0], axis=0)
            for first, last in ranges:
                change = jnp.dot(near[first:last], b00, preferred_element_type=jnp.float32)
                change += jnp.dot(near[first:last], b11, preferred_element_type=jnp.float32)
                change += jnp.dot(far[first:last], b20, preferred_element_type=jnp.float32)
                work[first:last, cols] -= change
            work[at, cols] = solved

        start, tiles = low, 0
        if k + 1 < blocks:
            column(start, BLOCK)
            start += BLOCK
            rows = diagonal_rows(k + 1)
        if start % 256:
            column(start, BLOCK)
            start += BLOCK
        tiles = (size + width - start) // 256

        if k + 1 < blocks:
            beside = min(tiles, pairs)

            def body(i, rows, start=start, column=column):
                column(pl.multiple_of(start + i * 256, 256), 256)
                return two_steps(rows)

            rows = lax.fori_loop(0, beside, body, rows)
            rows = lax.fori_loop(beside, pairs, lambda _, rows: two_steps(rows), rows)
        else:
            beside = 0

        @pl.loop(beside, tiles)
        def _(i, start=start, column=column):
            column(pl.multiple_of(start + i * 256, 256), 256)

    @pl.loop(0, size // 32)
    def _(i):
        at = pl.ds(pl.multiple_of(i * 32, 32), 32)
        out_ref[at, :] = work[at, size:].astype(out_ref.dtype)


def damped_solve(inner, target):
    size, width = inner.shape[0], target.shape[1]
    return pl.pallas_call(
        solve_kernel,
        out_shape=jax.ShapeDtypeStruct((size, width), jnp.bfloat16),
        in_specs=[pl.BlockSpec(memory_space=pltpu.VMEM)] * 2,
        out_specs=pl.BlockSpec(memory_space=pltpu.VMEM),
        scratch_shapes=[
            pltpu.VMEM((size, size + width), jnp.float32),
            pltpu.VMEM((size, 2 * BLOCK), jnp.bfloat16),
            pltpu.VMEM((size, 2 * BLOCK), jnp.bfloat16),
        ],
        compiler_params=pltpu.CompilerParams(vmem_limit_bytes=48 * 2**20),
        cost_estimate=pl.CostEstimate(
            flops=6 * size * size * width, bytes_accessed=10 * size * width, transcendentals=0
        ),
    )(inner, target)


def split_target(cross_gram, down_part):
    cross_high = lax.optimization_barrier(cross_gram.astype(jnp.bfloat16))
    cross_low = (cross_gram - cross_high.astype(jnp.float32)).astype(jnp.bfloat16)
    high_part = jnp.dot(cross_high, down_part, preferred_element_type=jnp.float32)
    low_part = jnp.dot(cross_low, down_part, preferred_element_type=jnp.float32)
    return high_part + low_part


def both_halves(value, core):
    other = lax.ppermute(value, "core", [(0, 1), (1, 0)])
    return jnp.where(
        core == 0,
        jnp.concatenate([value, other], axis=1),
        jnp.concatenate([other, value], axis=1),
    )


def local(
    stream,
    attn_gain,
    routes,
    route_weights,
    segment_ids,
    gate_weight,
    up_weight,
    down_weight,
    keep_channels,
    next_gain,
    kv_down,
    rope_down,
    kv_gain,
):
    f32, bf16 = jnp.float32, jnp.bfloat16
    tok_rows = stream.shape[0]
    chips = lax.axis_size(CHIPS)
    devices = 2 * chips
    experts = chips
    capacity = max(2, 3 * tok_rows * TOP // (2 * experts))
    core = lax.axis_index("core")
    expert_id = lax.axis_index(CHIPS)
    stream_f = stream.astype(f32)
    moe_input = rms_rows(stream_f, attn_gain).astype(bf16)
    half_width = down_weight.shape[2]
    model_width = stream.shape[1]

    gathered = lax.all_gather(moe_input, CHIPS, tiled=True).reshape(chips, tok_rows, model_width)
    gate_full = both_halves(gate_weight[0], core)
    up_full = both_halves(up_weight[0], core)

    token_total = tok_rows * devices
    seq_length = min(2048, token_total // 2)
    sequences = 2 * token_total // seq_length
    seq_hits = segment_ids[:, None] == jnp.arange(sequences, dtype=jnp.int32)[None, :]
    local_counts = jnp.sum(seq_hits.astype(f32), axis=0)
    count_row = jnp.pad(local_counts, (0, tok_rows - sequences))[None, :]
    packed_routes = jnp.concatenate([routes.T.astype(f32), route_weights.T, count_row], axis=0)
    all_routes = lax.all_gather(packed_routes, DEVICES)
    chosen = all_routes[:, :TOP] == expert_id.astype(f32)
    weight_rows = jnp.sum(jnp.where(chosen, all_routes[:, TOP : 2 * TOP], 0.0), axis=1)
    hits = jnp.any(chosen, axis=1)
    token_order = jnp.arange(tok_rows, dtype=jnp.int32)
    earlier = (token_order[:, None] < token_order[None, :]).astype(bf16)
    slots = jnp.dot(hits.astype(bf16), earlier, preferred_element_type=f32)
    slots = jnp.where(hits, slots, -1.0)
    slot_ids = jnp.arange(capacity, dtype=jnp.int32).astype(f32)
    by_core = slots.reshape(chips, 2, tok_rows)
    slots_mine = lax.dynamic_index_in_dim(by_core, core, 1, keepdims=False)
    slots_other = lax.dynamic_index_in_dim(by_core, 1 - core, 1, keepdims=False)
    weights_by_core = weight_rows.reshape(chips, 2, tok_rows)

    pick = (slots_mine[:, None, :] == slot_ids[None, :, None]).astype(bf16)
    picked = jnp.einsum("bct,btd->bcd", pick, gathered, preferred_element_type=f32).astype(bf16)
    picked = picked.reshape(chips * capacity, model_width)
    gate_proj = jnp.dot(picked, gate_full, preferred_element_type=f32)
    up_proj = jnp.dot(picked, up_full, preferred_element_type=f32)
    hidden_mine = (jax.nn.silu(gate_proj) * up_proj).astype(bf16)
    hidden_other = lax.ppermute(hidden_mine, "core", [(0, 1), (1, 0)])

    kept_index = lax.dynamic_slice_in_dim(keep_channels, expert_id, 1, 0)[0]
    unit_ids = jnp.arange(hidden_mine.shape[1], dtype=jnp.int32)
    select = (unit_ids[:, None] == kept_index[None, :]).astype(bf16)
    kept_mine = jnp.dot(hidden_mine, select, preferred_element_type=f32).astype(bf16)
    kept_other = jnp.dot(hidden_other, select, preferred_element_type=f32).astype(bf16)
    contract = (((0,), (0,)), ((), ()))
    gram = functools.partial(
        lax.dot_general, dimension_numbers=contract, preferred_element_type=f32
    )
    cross_gram = gram(kept_mine, hidden_mine) + gram(kept_other, hidden_other)
    inner_gram = gram(kept_mine, kept_mine) + gram(kept_other, kept_other)
    target_cols = split_target(cross_gram, down_weight[0])
    pruned = damped_solve(inner_gram, target_cols)

    def weighted(kept, slot_rows, weights):
        refit = jnp.dot(kept, pruned, preferred_element_type=f32).astype(bf16)
        place = slot_rows[:, None, :] == slot_ids[None, :, None]
        slot_weights = jnp.sum(jnp.where(place, weights[:, None, :], 0.0), axis=2)
        rows = refit.astype(f32) * slot_weights.reshape(-1)[:, None]
        return rows.astype(bf16).reshape(chips, capacity, half_width)

    weights_mine = lax.dynamic_index_in_dim(weights_by_core, core, 1, keepdims=False)
    weights_other = lax.dynamic_index_in_dim(weights_by_core, 1 - core, 1, keepdims=False)
    rows_mine = weighted(kept_mine, slots_mine, weights_mine)
    rows_other = weighted(kept_other, slots_other, weights_other)
    outgoing = jnp.stack(
        [jnp.where(core == 0, rows_mine, rows_other), jnp.where(core == 0, rows_other, rows_mine)],
        axis=1,
    ).reshape(devices, capacity, half_width)
    returned = lax.all_to_all(outgoing, DEVICES, split_axis=0, concat_axis=0, tiled=True)
    returned = returned.reshape(experts, 2, capacity, half_width)
    expert_range = jnp.arange(experts, dtype=jnp.int32)
    local_hits = jnp.any(routes[:, :, None] == expert_range[None, None, :], axis=1)
    local_slots = jnp.dot(earlier.T, local_hits.astype(bf16), preferred_element_type=f32)
    local_slots = jnp.where(local_hits, local_slots, -1.0)
    combine = (local_slots[:, :, None] == slot_ids[None, None, :]).astype(bf16)
    moe_sum = jnp.einsum("tec,ehcd->thd", combine, returned, preferred_element_type=f32)
    moe_out = moe_sum.reshape(tok_rows, model_width).astype(bf16)

    counts = jnp.sum(all_routes[:, 2 * TOP, :sequences], axis=0)
    sequence_range = jnp.arange(sequences, dtype=jnp.int32)
    before = sequence_range[None, :] < sequence_range[:, None]
    starts = jnp.sum(jnp.where(before, counts[None, :], 0.0), axis=1)
    token_start = jnp.sum(jnp.where(seq_hits, starts[None, :], 0.0), axis=1)
    global_index = (
        lax.axis_index(DEVICES) * tok_rows + jnp.arange(tok_rows, dtype=jnp.int32)
    ).astype(f32)
    position = global_index - token_start

    next_stream = (stream_f + moe_out.astype(f32)).astype(bf16)
    normed = rms_rows(next_stream.astype(f32), next_gain).astype(bf16)
    compressed = jnp.dot(normed, kv_down, preferred_element_type=f32)
    latent = rms_rows(compressed, kv_gain).astype(bf16)
    rope_in = jnp.dot(normed, rope_down, preferred_element_type=f32)
    rope_key = rotate(rope_in, position).astype(bf16)
    return (moe_out, latent, rope_key)


def solution(mesh):
    chips_mesh = Mesh(
        mesh.devices.reshape(mesh.shape["expert"], mesh.shape["mp"] // 2, 2), DEVICES
    )
    split = P(DEVICES)
    in_specs = (split, P(), split, split, split, split, split, split, P(), P(), P(), P(), P())
    return jax.shard_map(
        local, mesh=chips_mesh, in_specs=in_specs, out_specs=(split,) * 3, check_vma=False
    )
```
